512 devices in a mesh: dp: 128 (over z, y_lo, x), pair: 4 (over y_hi, core).
Axes of the slice: x: 4, y: 4 (y_hi: 2, y_lo: 2; y = y_hi * 2 + y_lo), z: 16, core: 2. Of those that a mesh axis runs over, the one named last changes fastest.
Arguments:
- images: bfloat16 [229376, 1152], P(('dp', 'pair')), may hold values from -0.59765625 to 0.59765625
- texts: bfloat16 [229376, 1152], P(('dp', 'pair')), may hold values from -0.59765625 to 0.59765625
- labels: int32 [229376], P(('dp', 'pair')), may hold values from 0 to 229375, as said below
- log_scale: float32 [1], replicated, may hold values from 1.8 to 2.6
- bias: float32 [1], replicated, may hold values from -8 to -4
Outputs:
- image_grad: bfloat16 [229376, 1152], P(('dp', 'pair'))
- text_grad: bfloat16 [229376, 1152], P(('dp', 'pair'))
The draws below stay inside these ranges and needn't reach their ends.
Inputs may be any that keep to these rules, and one draw needn't show every extreme that they name: `labels`: each image's matching text lies in its own block (row // 448) or in block (row // 448) xor m for one of m = 1, 4, 8, 256; each image has exactly one match.
All inputs are finite; a program needn't handle non-finite values.
Results may differ from the reference program's by a relative error of at most 0.0039.
Values may be sent and summed in bfloat16 or wider, within the bound.
No kernel may reach another device: no remote copies, remote signals or barrier semaphores. Data moves between devices by JAX's collectives and lax.ppermute only.
A program may use at most 64 MiB of HBM per device.

```python
import jax
import jax.numpy as jnp
from jax import lax

D = 1152
B = 448
BLOCKS = 512
PAIRS = 229376
FAR1 = 4
FAR2 = 8
FAR3 = 256


def draw_labels(key, part):
    key = jax.random.fold_in(key, 11)
    key_pick, key_row = jax.random.split(key)
    offsets = jnp.array([0, 1, FAR1, FAR2, FAR3], dtype=jnp.int32)
    pick = jax.random.randint(key_pick, (BLOCKS, B), 0, 5)
    blocks = jnp.arange(BLOCKS, dtype=jnp.int32)[:, None]
    partner = jnp.bitwise_xor(blocks, offsets[pick])
    within = jax.random.randint(key_row, (BLOCKS, B), 0, B)
    flat = (partner * B + within).reshape(PAIRS).astype(jnp.int32)
    rows = jnp.arange(PAIRS, dtype=jnp.int32)
    flat = jnp.where(rows == 0, 0, flat)
    flat = jnp.where(rows == PAIRS - 1, PAIRS - 1, flat)
    return flat


def block_scale(key, dims, cuts, low, high):
    def one(axis_at, parts):
        heights = jax.random.uniform(jax.random.fold_in(jax.random.fold_in(key, 6), axis_at), (parts,), jnp.float32, low / len(cuts), high / len(cuts))
        return jnp.repeat(jnp.exp(heights), dims[axis_at] // parts).reshape((-1,) + (1,) * (len(dims) - axis_at - 1))

    gain = one(*cuts[0])
    for cut in cuts[1:]:
        gain = gain * one(*cut)
    return gain


def centred(stream_key, dims, spread, most, cuts=(), kind=jnp.bfloat16):
    drawn = spread * jax.random.normal(stream_key, dims, jnp.float32)
    if cuts:
        drawn = drawn * block_scale(stream_key, dims, cuts, -0.22, 0.18)
    return jnp.clip(drawn, -most, most).astype(kind)


def setup_inputs(seed: int = 0) -> dict:
    splits = jax.random.split(jax.random.key(seed), 6)
    images = centred(splits[0], (PAIRS, D), 0.1, 0.59765625, ((0, 512),))
    texts = centred(splits[1], (PAIRS, D), 0.1, 0.59765625, ((0, 512),))
    labels = draw_labels(jax.random.fold_in(splits[5], 71), 0)
    log_scale = jnp.clip(jax.random.uniform(splits[3], (1,), jnp.float32, 1.8, 2.6), 1.8, 2.6)
    bias = jnp.clip(jax.random.uniform(splits[4], (1,), jnp.float32, -8.0, -4.0), -8.0, -4.0)
    return {"images": images, "texts": texts, "labels": labels, "log_scale": log_scale, "bias": bias}


def reference(images, texts, labels, log_scale, bias):
    scale = jnp.exp(log_scale[0])
    shift = bias[0]
    img_blocks = images.reshape(BLOCKS, B, D).astype(jnp.float32)
    txt_blocks = texts.reshape(BLOCKS, B, D).astype(jnp.float32)
    lab_blocks = labels.reshape(BLOCKS, B)
    blocks = jnp.arange(BLOCKS, dtype=jnp.int32)
    columns = jnp.arange(B, dtype=jnp.int32)
    img_acc = jnp.zeros((BLOCKS, B, D), jnp.float32)
    txt_acc = jnp.zeros((BLOCKS, B, D), jnp.float32)
    for offset in (0, 1, FAR1, FAR2, FAR3):
        partner = jnp.bitwise_xor(blocks, offset).astype(jnp.int32)
        their_txt = txt_blocks[partner]
        logits = scale * jnp.einsum("gid,gjd->gij", img_blocks, their_txt) + shift
        target = (lab_blocks[:, :, None] == (partner[:, None, None] * B + columns[None, None, :])).astype(jnp.float32)
        coeff = (jax.nn.sigmoid(logits) - target).astype(jnp.bfloat16)
        coeff = lax.optimization_barrier(coeff).astype(jnp.float32)
        img_acc = img_acc + jnp.einsum("gij,gjd->gid", coeff, their_txt)
        terms = jnp.einsum("gij,gid->gjd", coeff, img_blocks)
        txt_acc = txt_acc + terms[partner]
    image_grad = (scale * img_acc).reshape(PAIRS, D).astype(jnp.bfloat16)
    text_grad = (scale * txt_acc).reshape(PAIRS, D).astype(jnp.bfloat16)
    return image_grad, text_grad
```

```python
import functools

import jax
import jax.numpy as jnp
from jax import lax
from jax.experimental import pallas as pl
from jax.experimental.pallas import tpu as pltpu
from jax.sharding import PartitionSpec as P

VMEM = pl.BlockSpec(memory_space=pltpu.VMEM)
SMEM = pl.BlockSpec(memory_space=pltpu.SMEM)
DIGIT_ROWS = 16


def from_partner(block, axis, bit):
    count = lax.axis_size(axis)
    return lax.ppermute(block, axis, [(i, i ^ (1 << bit)) for i in range(count)])


def gradient(rows, cols, hit, scale, shift):
    logits = scale * lax.dot_general(
        rows, cols, (((1,), (1,)), ((), ())), preferred_element_type=jnp.float32
    ) + shift
    coeff = (jax.nn.sigmoid(logits) - hit.astype(jnp.float32)).astype(jnp.bfloat16)
    return jnp.dot(coeff, cols, preferred_element_type=jnp.float32)


def hit_columns(label_column, base, count):
    return label_column - base == lax.broadcasted_iota(jnp.int32, (count, count), 1)


def hit_rows(label_row, base, count):
    return label_row - base == lax.broadcasted_iota(jnp.int32, (count, count), 0)


def label_row_of(digit_rows, count):
    d = digit_rows[:, :count].astype(jnp.float32)
    return (d[0:1] + 256.0 * d[1:2] + 65536.0 * d[2:3]).astype(jnp.int32)


def first_kernel(scalars, bases, img, txt, lab_col, lab_row, far_txt, img_acc, txt_acc):
    count = img.shape[0]
    scale, shift = scalars[0], scalars[1]
    img_acc[...] = gradient(img[...], far_txt[...], hit_columns(lab_col[...], bases[4], count), scale, shift)
    img_acc[...] += gradient(img[...], txt[...], hit_columns(lab_col[...], bases[0], count), scale, shift)
    txt_acc[...] = gradient(txt[...], img[...], hit_rows(lab_row[...], bases[0], count), scale, shift)


def near_kernel(which, last, scalars, bases, img, txt, lab_col, packed, img_in, txt_in, img_out, txt_out):
    count = img.shape[0]
    scale, shift = scalars[0], scalars[1]
    their_txt = packed[:count, :]
    their_img = packed[count : 2 * count, :]
    their_lab = label_row_of(packed[2 * count :, :], count)
    total = img_in[...] + gradient(
        img[...], their_txt, hit_columns(lab_col[...], bases[which], count), scale, shift
    )
    img_out[...] = (scale * total).astype(jnp.bfloat16) if last else total
    txt_out[...] = txt_in[...] + gradient(
        txt[...], their_img, hit_rows(their_lab, bases[0], count), scale, shift
    )


def last_kernel(scalars, bases, txt, packed, txt_in, image_grad, text_grad, image_grad_out):
    count = txt.shape[0]
    scale, shift = scalars[0], scalars[1]
    their_lab = label_row_of(packed[count:, :], count)
    total = txt_in[...] + gradient(
        txt[...], packed[:count, :], hit_rows(their_lab, bases[0], count), scale, shift
    )
    text_grad[...] = (scale * total).astype(jnp.bfloat16)


def cost(products, count, width):
    return pl.CostEstimate(
        flops=4 * products * count * count * width,
        bytes_accessed=6 * products * count * width,
        transcendentals=products * count * count,
    )


def local(images, texts, labels, log_scale, bias):
    count, width = images.shape
    pair_size = lax.axis_size("pair")
    far = lax.axis_size("dp").bit_length() - 2
    myself = lax.axis_index("dp") * pair_size + lax.axis_index("pair")

    far_txt = from_partner(texts, "dp", far)

    digits = jnp.stack([labels & 255, (labels >> 8) & 255, labels >> 16]).astype(jnp.bfloat16)
    digits = jnp.pad(digits, ((0, DIGIT_ROWS - 3), (0, width - count)))
    packed = jnp.concatenate([texts, images, digits], axis=0)
    near = [("pair", 0, 1), ("dp", 0, pair_size), ("dp", 1, 2 * pair_size)]
    arrived = [from_partner(packed, axis, bit) for axis, bit, _ in near]
    far_img = from_partner(jnp.concatenate([images, digits], axis=0), "dp", far)

    offsets = jnp.array([0, 1, pair_size, 2 * pair_size, pair_size << far], jnp.int32)
    bases = jnp.bitwise_xor(myself, offsets) * count
    scalars = jnp.concatenate([jnp.exp(log_scale), bias])
    lab_col = labels.reshape(count, 1)
    lab_row = labels.reshape(1, count)
    params = pltpu.CompilerParams(vmem_limit_bytes=48 << 20)
    acc = jax.ShapeDtypeStruct((count, width), jnp.float32)
    out = jax.ShapeDtypeStruct((count, width), jnp.bfloat16)

    img_acc, txt_acc = pl.pallas_call(
        first_kernel,
        out_shape=(acc, acc),
        in_specs=[SMEM, SMEM] + [VMEM] * 5,
        out_specs=(VMEM, VMEM),
        compiler_params=params,
        cost_estimate=cost(3, count, width),
        name="own_and_far_texts",
    )(scalars, bases, images, texts, lab_col, lab_row, far_txt)
    for at, got in enumerate(arrived):
        last = at == len(arrived) - 1
        img_acc, txt_acc = pl.pallas_call(
            functools.partial(near_kernel, at + 1, last),
            out_shape=(out if last else acc, acc),
            in_specs=[SMEM, SMEM] + [VMEM] * 6,
            out_specs=(VMEM, VMEM),
            compiler_params=params,
            cost_estimate=cost(2, count, width),
            name="near_partner",
        )(scalars, bases, images, texts, lab_col, got, img_acc, txt_acc)
    text_grad, image_grad = pl.pallas_call(
        last_kernel,
        out_shape=(out, out),
        in_specs=[SMEM, SMEM] + [VMEM] * 3 + [pl.BlockSpec(memory_space=pl.ANY)],
        out_specs=(VMEM, pl.BlockSpec(memory_space=pl.ANY)),
        input_output_aliases={5: 1},
        compiler_params=params,
        cost_estimate=cost(1, count, width),
        name="far_images",
    )(scalars, bases, texts, far_img, txt_acc, img_acc)
    return image_grad, text_grad


def solution(mesh):
    placed = (P(("dp", "pair"), None), P(("dp", "pair"), None), P(("dp", "pair")), P(), P())
    return jax.shard_map(
        local,
        mesh=mesh,
        in_specs=placed,
        out_specs=(P(("dp", "pair"), None), P(("dp", "pair"), None)),
        check_vma=False,
    )
```

```python
import jax
import jax.numpy as jnp
from jax import lax
from jax.experimental import pallas as pl
from jax.experimental.pallas import tpu as pltpu
from jax.sharding import PartitionSpec as P

VMEM = pl.BlockSpec(memory_space=pltpu.VMEM)
SMEM = pl.BlockSpec(memory_space=pltpu.SMEM)
DIGIT_ROWS = 16
CHUNKS = 2


def from_partner(block, axis, bit):
    count = lax.axis_size(axis)
    return lax.ppermute(block, axis, [(i, i ^ (1 << bit)) for i in range(count)])


def gradient(rows, cols, hit, scale, shift):
    logits = scale * lax.dot_general(
        rows, cols, (((1,), (1,)), ((), ())), preferred_element_type=jnp.float32
    ) + shift
    coeff = (jax.nn.sigmoid(logits) - hit.astype(jnp.float32)).astype(jnp.bfloat16)
    return jnp.dot(coeff, cols, preferred_element_type=jnp.float32)


def hit_columns(label_column, base, count, chunk):
    return label_column - base == lax.broadcasted_iota(jnp.int32, (count, chunk), 1)


def hit_rows(label_row, base, count, chunk):
    return label_row - base == lax.broadcasted_iota(jnp.int32, (count, chunk), 0)


def label_row_of(digit_rows, count):
    d = digit_rows[:, :count].astype(jnp.float32)
    return (d[0:1] + 256.0 * d[1:2] + 65536.0 * d[2:3]).astype(jnp.int32)


def own_kernel(scalars, bases, img, txt, lab_col, lab_row, img_acc, txt_acc):
    count = img.shape[0]
    scale, shift = scalars[0], scalars[1]
    img_acc[...] = gradient(img[...], txt[...], hit_columns(lab_col[...], bases[0], count, count), scale, shift)
    txt_acc[...] = gradient(txt[...], img[...], hit_rows(lab_row[...], bases[0], count, count), scale, shift)


def near_kernel(bases, scalars, img, txt, lab_col, near1, near2, near3, img_in, txt_in, img_out, txt_out):
    count = img.shape[0]
    chunk = (near1.shape[0] - DIGIT_ROWS) // 2
    scale, shift = scalars[0], scalars[1]
    img_total, txt_total = img_in[...], txt_in[...]
    for which, near in ((1, near1), (2, near2), (3, near3)):
        hit = hit_columns(lab_col[...], bases[which] + bases[5], count, chunk)
        img_total += gradient(img[...], near[:chunk, :], hit, scale, shift)
        hit = hit_rows(label_row_of(near[2 * chunk :, :], chunk), bases[0], count, chunk)
        txt_total += gradient(txt[...], near[chunk : 2 * chunk, :], hit, scale, shift)
    img_out[...] = img_total
    txt_out[...] = txt_total


def far_texts_kernel(scalars, bases, img, lab_col, far_txt, img_in, image_grad):
    count = img.shape[0]
    scale, shift = scalars[0], scalars[1]
    hit = hit_columns(lab_col[...], bases[4], count, count)
    total = img_in[...] + gradient(img[...], far_txt[...], hit, scale, shift)
    image_grad[...] = (scale * total).astype(jnp.bfloat16)


def far_images_kernel(scalars, bases, txt, packed, txt_in, image_grad, text_grad, image_grad_out):
    count = txt.shape[0]
    scale, shift = scalars[0], scalars[1]
    hit = hit_rows(label_row_of(packed[count:, :], count), bases[0], count, count)
    total = txt_in[...] + gradient(txt[...], packed[:count, :], hit, scale, shift)
    text_grad[...] = (scale * total).astype(jnp.bfloat16)


def cost(products, count, width):
    return pl.CostEstimate(
        flops=4 * products * count * count * width,
        bytes_accessed=6 * products * count * width,
        transcendentals=products * count * count,
    )


def local(images, texts, labels, log_scale, bias):
    count, width = images.shape
    pair_size = lax.axis_size("pair")
    far = lax.axis_size("dp").bit_length() - 2
    myself = lax.axis_index("dp") * pair_size + lax.axis_index("pair")

    anywhere = pl.BlockSpec(memory_space=pl.ANY)
    params = pltpu.CompilerParams(vmem_limit_bytes=48 << 20)
    acc = jax.ShapeDtypeStruct((count, width), jnp.float32)
    out = jax.ShapeDtypeStruct((count, width), jnp.bfloat16)

    def kernel(body, out_shape, *args, passed=None, products=1):
        many = isinstance(out_shape, tuple)
        specs = [SMEM, SMEM] + [VMEM] * (len(args) - 2)
        out_specs = (VMEM,) * len(out_shape) if many else VMEM
        aliases = {}
        if passed is not None:
            specs[-1] = anywhere
            out_specs = out_specs[:-1] + (anywhere,)
            aliases = {len(args) - 1: len(out_shape) - 1}
        return pl.pallas_call(
            body,
            out_shape=out_shape,
            in_specs=specs,
            out_specs=out_specs,
            input_output_aliases=aliases,
            compiler_params=params,
            cost_estimate=cost(products, count, width),
            name=body.__name__,
        )(*args)

    digits = jnp.stack([labels & 255, (labels >> 8) & 255, labels >> 16]).astype(jnp.bfloat16)
    digits = jnp.pad(digits, ((0, DIGIT_ROWS - 3), (0, width - count)))
    far_txt = from_partner(texts, "dp", far)
    far_img = from_partner(jnp.concatenate([images, digits], axis=0), "dp", far)

    offsets = jnp.array([0, 1, pair_size, 2 * pair_size, pair_size << far], jnp.int32)
    bases = jnp.bitwise_xor(myself, offsets) * count
    scalars = jnp.concatenate([jnp.exp(log_scale), bias])
    lab_col = labels.reshape(count, 1)
    lab_row = labels.reshape(1, count)

    sums = kernel(own_kernel, (acc, acc), scalars, bases, images, texts, lab_col, lab_row, products=2)
    chunk = count // CHUNKS

    def near(step, sums):
        at = step * chunk
        part = jnp.concatenate(
            [
                lax.dynamic_slice_in_dim(texts, at, chunk, 0),
                lax.dynamic_slice_in_dim(images, at, chunk, 0),
                jnp.pad(
                    lax.dynamic_slice_in_dim(digits, at, chunk, 1), ((0, 0), (0, width - chunk))
                ),
            ],
            axis=0,
        )
        arrived = [from_partner(part, axis, bit) for axis, bit in (("dp", 1), ("dp", 0), ("pair", 0))]
        here = jnp.concatenate([bases, jnp.reshape(at, (1,))])
        return kernel(
            near_kernel, (acc, acc), here, scalars, images, texts, lab_col, *arrived[::-1], *sums, products=3
        )

    img_acc, txt_acc = lax.fori_loop(0, CHUNKS, near, sums)
    image_grad = kernel(far_texts_kernel, out, scalars, bases, images, lab_col, far_txt, img_acc)
    text_grad, image_grad = kernel(
        far_images_kernel, (out, out), scalars, bases, texts, far_img, txt_acc, image_grad, passed=image_grad
    )
    return image_grad, text_grad


def solution(mesh):
    placed = (P(("dp", "pair"), None), P(("dp", "pair"), None), P(("dp", "pair")), P(), P())
    return jax.shard_map(
        local,
        mesh=mesh,
        in_specs=placed,
        out_specs=(P(("dp", "pair"), None), P(("dp", "pair"), None)),
        check_vma=False,
    )
```

```python
import jax
import jax.numpy as jnp
from jax import lax
from jax.experimental import pallas as pl
from jax.experimental.pallas import tpu as pltpu
from jax.sharding import PartitionSpec as P

VMEM = pl.BlockSpec(memory_space=pltpu.VMEM)
SMEM = pl.BlockSpec(memory_space=pltpu.SMEM)
DIGIT_ROWS = 16
CHUNKS = 2
VMEM_LIMIT = 28 << 20


def from_partner(block, axis, bit):
    count = lax.axis_size(axis)
    return lax.ppermute(block, axis, [(i, i ^ (1 << bit)) for i in range(count)])


def gradient(rows, cols, hit, scale, shift):
    logits = scale * lax.dot_general(
        rows, cols, (((1,), (1,)), ((), ())), preferred_element_type=jnp.float32
    ) + shift
    coeff = (jax.nn.sigmoid(logits) - hit.astype(jnp.float32)).astype(jnp.bfloat16)
    return jnp.dot(coeff, cols, preferred_element_type=jnp.float32)


def hit_columns(label_column, base, count, chunk):
    return label_column - base == lax.broadcasted_iota(jnp.int32, (count, chunk), 1)


def hit_rows(label_row, base, count, chunk):
    return label_row - base == lax.broadcasted_iota(jnp.int32, (count, chunk), 0)


def label_row_of(digit_rows, count):
    d = digit_rows[:, :count].astype(jnp.float32)
    return (d[0:1] + 256.0 * d[1:2] + 65536.0 * d[2:3]).astype(jnp.int32)


def own_kernel(scalars, bases, img, txt, lab_col, lab_row, img_acc, txt_acc, lab_out):
    count = img.shape[0]
    scale, shift = scalars[0], scalars[1]
    img_acc[...] = gradient(img[...], txt[...], hit_columns(lab_col[...], bases[0], count, count), scale, shift)
    txt_acc[...] = gradient(txt[...], img[...], hit_rows(lab_row[...], bases[0], count, count), scale, shift)
    lab_out[...] = lab_row[...]


def near_kernel(bases, scalars, img, txt, lab_col, near1, near2, near3, img_in, txt_in, far_lab, img_out, txt_out):
    count = img.shape[0]
    chunk = (near1.shape[0] - DIGIT_ROWS) // 2
    scale, shift = scalars[0], scalars[1]
    img_total, txt_total = img_in[...], txt_in[...]
    for which, near in ((1, near1), (2, near2), (3, near3)):
        hit = hit_columns(lab_col[...], bases[which] + bases[5], count, chunk)
        img_total += gradient(img[...], near[:chunk, :], hit, scale, shift)
        hit = hit_rows(label_row_of(near[2 * chunk :, :], chunk), bases[0], count, chunk)
        txt_total += gradient(txt[...], near[chunk : 2 * chunk, :], hit, scale, shift)
    img_out[...] = img_total
    txt_out[...] = txt_total


def far_texts_kernel(scalars, bases, img, lab_col, far_txt, img_in, image_grad):
    count = img.shape[0]
    scale, shift = scalars[0], scalars[1]
    hit = hit_columns(lab_col[...], bases[4], count, count)
    total = img_in[...] + gradient(img[...], far_txt[...], hit, scale, shift)
    image_grad[...] = (scale * total).astype(jnp.bfloat16)


def far_images_kernel(scalars, bases, txt, far_img, far_lab, txt_in, image_grad, text_grad, image_grad_out):
    count = txt.shape[0]
    scale, shift = scalars[0], scalars[1]
    hit = hit_rows(far_lab[...], bases[0], count, count)
    total = txt_in[...] + gradient(txt[...], far_img[...], hit, scale, shift)
    text_grad[...] = (scale * total).astype(jnp.bfloat16)


def cost(products, count, width):
    return pl.CostEstimate(
        flops=4 * products * count * count * width,
        bytes_accessed=6 * products * count * width,
        transcendentals=products * count * count,
    )


def local(images, texts, labels, log_scale, bias):
    count, width = images.shape
    pair_size = lax.axis_size("pair")
    far = lax.axis_size("dp").bit_length() - 2
    myself = lax.axis_index("dp") * pair_size + lax.axis_index("pair")

    anywhere = pl.BlockSpec(memory_space=pl.ANY)
    params = pltpu.CompilerParams(vmem_limit_bytes=VMEM_LIMIT)
    acc = jax.ShapeDtypeStruct((count, width), jnp.float32)
    out = jax.ShapeDtypeStruct((count, width), jnp.bfloat16)

    def kernel(body, out_shape, *args, passed=None, products=1):
        many = isinstance(out_shape, tuple)
        specs = [SMEM, SMEM] + [VMEM] * (len(args) - 2)
        out_specs = (VMEM,) * len(out_shape) if many else VMEM
        aliases = {}
        if passed is not None:
            specs[-1] = anywhere
            out_specs = out_specs[:-1] + (anywhere,)
            aliases = {len(args) - 1: len(out_shape) - 1}
        return pl.pallas_call(
            body,
            out_shape=out_shape,
            in_specs=specs,
            out_specs=out_specs,
            input_output_aliases=aliases,
            compiler_params=params,
            cost_estimate=cost(products, count, width),
            name=body.__name__,
        )(*args)

    digits = jnp.stack([labels & 255, (labels >> 8) & 255, labels >> 16]).astype(jnp.bfloat16)
    digits = jnp.pad(digits, ((0, DIGIT_ROWS - 3), (0, width - count)))
    far_txt = from_partner(texts, "dp", far)
    far_img = from_partner(images, "dp", far)

    offsets = jnp.array([0, 1, pair_size, 2 * pair_size, pair_size << far], jnp.int32)
    bases = jnp.bitwise_xor(myself, offsets) * count
    scalars = jnp.concatenate([jnp.exp(log_scale), bias])
    lab_col = labels.reshape(count, 1)
    lab_row = labels.reshape(1, count)

    lab = jax.ShapeDtypeStruct((1, count), jnp.int32)
    *sums, lab_sent = kernel(
        own_kernel, (acc, acc, lab), scalars, bases, images, texts, lab_col, lab_row, products=2
    )
    far_lab = from_partner(lab_sent, "dp", far)
    chunk = count // CHUNKS

    def near(step, sums):
        at = step * chunk
        part = jnp.concatenate(
            [
                lax.dynamic_slice_in_dim(texts, at, chunk, 0),
                lax.dynamic_slice_in_dim(images, at, chunk, 0),
                jnp.pad(
                    lax.dynamic_slice_in_dim(digits, at, chunk, 1), ((0, 0), (0, width - chunk))
                ),
            ],
            axis=0,
        )
        arrived = [from_partner(part, axis, bit) for axis, bit in (("dp", 1), ("dp", 0), ("pair", 0))]
        here = jnp.concatenate([bases, jnp.reshape(at, (1,))])
        return kernel(
            near_kernel, (acc, acc), here, scalars, images, texts, lab_col, *arrived[::-1], *sums, far_lab, products=3
        )

    img_acc, txt_acc = lax.fori_loop(0, CHUNKS, near, tuple(sums))
    image_grad = kernel(far_texts_kernel, out, scalars, bases, images, lab_col, far_txt, img_acc)
    text_grad, image_grad = kernel(
        far_images_kernel, (out, out), scalars, bases, texts, far_img, far_lab, txt_acc, image_grad, passed=image_grad
    )
    return image_grad, text_grad


def solution(mesh):
    placed = (P(("dp", "pair"), None), P(("dp", "pair"), None), P(("dp", "pair")), P(), P())
    return jax.shard_map(
        local,
        mesh=mesh,
        in_specs=placed,
        out_specs=(P(("dp", "pair"), None), P(("dp", "pair"), None)),
        check_vma=False,
    )
```

```python
import jax
import jax.numpy as jnp
from jax import lax
from jax.experimental import pallas as pl
from jax.experimental.pallas import tpu as pltpu
from jax.sharding import PartitionSpec as P

VMEM = pl.BlockSpec(memory_space=pltpu.VMEM)
SMEM = pl.BlockSpec(memory_space=pltpu.SMEM)
DIGIT_ROWS = 16
CHUNKS = 2
VMEM_LIMIT = 28 << 20


def from_partner(block, axis, bit):
    count = lax.axis_size(axis)
    return lax.ppermute(block, axis, [(i, i ^ (1 << bit)) for i in range(count)])


def gradient(rows, cols, hit, scale, shift):
    logits = scale * lax.dot_general(
        rows, cols, (((1,), (1,)), ((), ())), preferred_element_type=jnp.float32
    ) + shift
    coeff = (jax.nn.sigmoid(logits) - hit.astype(jnp.float32)).astype(jnp.bfloat16)
    return jnp.dot(coeff, cols, preferred_element_type=jnp.float32)


def hit_columns(label_column, base, count, chunk):
    return label_column - base == lax.broadcasted_iota(jnp.int32, (count, chunk), 1)


def hit_rows(label_row, base, count, chunk):
    return label_row - base == lax.broadcasted_iota(jnp.int32, (count, chunk), 0)


def label_row_of(digit_rows, count):
    d = digit_rows[:, :count].astype(jnp.float32)
    return (d[0:1] + 256.0 * d[1:2] + 65536.0 * d[2:3]).astype(jnp.int32)


def own_kernel(scalars, bases, img, txt, lab_col, lab_row, img_acc, txt_acc, lab_out):
    count = img.shape[0]
    scale, shift = scalars[0], scalars[1]
    img_acc[...] = gradient(img[...], txt[...], hit_columns(lab_col[...], bases[0], count, count), scale, shift)
    txt_acc[...] = gradient(txt[...], img[...], hit_rows(lab_row[...], bases[0], count, count), scale, shift)
    lab_out[...] = lab_row[...]


def near_kernel(bases, scalars, img, txt, lab_col, near1, near2, near3, img_in, txt_in, img_out, txt_out):
    count = img.shape[0]
    chunk = (near1.shape[0] - DIGIT_ROWS) // 2
    scale, shift = scalars[0], scalars[1]
    img_total, txt_total = img_in[...], txt_in[...]
    for which, near in ((1, near1), (2, near2), (3, near3)):
        hit = hit_columns(lab_col[...], bases[which] + bases[5], count, chunk)
        img_total += gradient(img[...], near[:chunk, :], hit, scale, shift)
        hit = hit_rows(label_row_of(near[2 * chunk :, :], chunk), bases[0], count, chunk)
        txt_total += gradient(txt[...], near[chunk : 2 * chunk, :], hit, scale, shift)
    img_out[...] = img_total
    txt_out[...] = txt_total


def far_texts_kernel(scalars, bases, img, lab_col, far_txt, img_in, image_grad):
    count = img.shape[0]
    scale, shift = scalars[0], scalars[1]
    hit = hit_columns(lab_col[...], bases[4], count, count)
    total = img_in[...] + gradient(img[...], far_txt[...], hit, scale, shift)
    image_grad[...] = (scale * total).astype(jnp.bfloat16)


def far_images_kernel(scalars, bases, txt, far_img, far_lab, txt_in, image_grad, text_grad, image_grad_out):
    count = txt.shape[0]
    scale, shift = scalars[0], scalars[1]
    hit = hit_rows(far_lab[...], bases[0], count, count)
    total = txt_in[...] + gradient(txt[...], far_img[...], hit, scale, shift)
    text_grad[...] = (scale * total).astype(jnp.bfloat16)


def cost(products, count, width):
    return pl.CostEstimate(
        flops=4 * products * count * count * width,
        bytes_accessed=6 * products * count * width,
        transcendentals=products * count * count,
    )


def local(images, texts, labels, log_scale, bias):
    count, width = images.shape
    pair_size = lax.axis_size("pair")
    far = lax.axis_size("dp").bit_length() - 2
    myself = lax.axis_index("dp") * pair_size + lax.axis_index("pair")

    anywhere = pl.BlockSpec(memory_space=pl.ANY)
    params = pltpu.CompilerParams(vmem_limit_bytes=VMEM_LIMIT)
    acc = jax.ShapeDtypeStruct((count, width), jnp.float32)
    out = jax.ShapeDtypeStruct((count, width), jnp.bfloat16)

    def kernel(body, out_shape, *args, passed=None, products=1):
        many = isinstance(out_shape, tuple)
        specs = [SMEM, SMEM] + [VMEM] * (len(args) - 2)
        out_specs = (VMEM,) * len(out_shape) if many else VMEM
        aliases = {}
        if passed is not None:
            specs[-1] = anywhere
            out_specs = out_specs[:-1] + (anywhere,)
            aliases = {len(args) - 1: len(out_shape) - 1}
        return pl.pallas_call(
            body,
            out_shape=out_shape,
            in_specs=specs,
            out_specs=out_specs,
            input_output_aliases=aliases,
            compiler_params=params,
            cost_estimate=cost(products, count, width),
            name=body.__name__,
        )(*args)

    digits = jnp.stack([labels & 255, (labels >> 8) & 255, labels >> 16]).astype(jnp.bfloat16)
    digits = jnp.pad(digits, ((0, DIGIT_ROWS - 3), (0, width - count)))
    far_txt = from_partner(texts, "dp", far)
    far_img = from_partner(images, "dp", far)

    offsets = jnp.array([0, 1, pair_size, 2 * pair_size, pair_size << far], jnp.int32)
    bases = jnp.bitwise_xor(myself, offsets) * count
    scalars = jnp.concatenate([jnp.exp(log_scale), bias])
    lab_col = labels.reshape(count, 1)
    lab_row = labels.reshape(1, count)

    lab = jax.ShapeDtypeStruct((1, count), jnp.int32)
    *sums, lab_sent = kernel(
        own_kernel, (acc, acc, lab), scalars, bases, images, texts, lab_col, lab_row, products=2
    )
    far_lab = from_partner(lab_sent, "dp", far)
    chunk = count // CHUNKS

    def near(step, sums):
        at = step * chunk
        part = jnp.concatenate(
            [
                lax.dynamic_slice_in_dim(texts, at, chunk, 0),
                lax.dynamic_slice_in_dim(images, at, chunk, 0),
                jnp.pad(
                    lax.dynamic_slice_in_dim(digits, at, chunk, 1), ((0, 0), (0, width - chunk))
                ),
            ],
            axis=0,
        )
        arrived = [from_partner(part, axis, bit) for axis, bit in (("dp", 1), ("dp", 0), ("pair", 0))]
        here = jnp.concatenate([bases, jnp.reshape(at, (1,))])
        return kernel(
            near_kernel, (acc, acc), here, scalars, images, texts, lab_col, *arrived[::-1], *sums, products=3
        )

    img_acc, txt_acc = lax.fori_loop(0, CHUNKS, near, tuple(sums))
    image_grad = kernel(far_texts_kernel, out, scalars, bases, images, lab_col, far_txt, img_acc)
    text_grad, image_grad = kernel(
        far_images_kernel, (out, out), scalars, bases, texts, far_img, far_lab, txt_acc, image_grad, passed=image_grad
    )
    return image_grad, text_grad


def solution(mesh):
    placed = (P(("dp", "pair"), None), P(("dp", "pair"), None), P(("dp", "pair")), P(), P())
    return jax.shard_map(
        local,
        mesh=mesh,
        in_specs=placed,
        out_specs=(P(("dp", "pair"), None), P(("dp", "pair"), None)),
        check_vma=False,
    )
```

```python
import jax
import jax.numpy as jnp
from jax import lax
from jax.experimental import pallas as pl
from jax.experimental.pallas import tpu as pltpu
from jax.sharding import PartitionSpec as P

VMEM = pl.BlockSpec(memory_space=pltpu.VMEM)
SMEM = pl.BlockSpec(memory_space=pltpu.SMEM)
DIGIT_ROWS = 16
CHUNKS = 2
RING = 16
FIRST_STEPS = 1
VMEM_LIMIT = 28 << 20


def from_partner(block, axis, bit):
    count = lax.axis_size(axis)
    return lax.ppermute(block, axis, [(i, i ^ (1 << bit)) for i in range(count)])


def along_ring(block, steps):
    axes = ("dp", "pair")
    count = lax.axis_size(axes)
    step = count // RING * steps
    return lax.ppermute(
        block, axes, [(i, (i + (step if i % 2 == 0 else -step)) % count) for i in range(count)]
    )


def gradient(rows, cols, hit, scale, shift):
    logits = scale * lax.dot_general(
        rows, cols, (((1,), (1,)), ((), ())), preferred_element_type=jnp.float32
    ) + shift
    coeff = (jax.nn.sigmoid(logits) - hit.astype(jnp.float32)).astype(jnp.bfloat16)
    return jnp.dot(coeff, cols, preferred_element_type=jnp.float32)


def hit_columns(label_column, base, count, chunk):
    return label_column - base == lax.broadcasted_iota(jnp.int32, (count, chunk), 1)


def hit_rows(label_row, base, count, chunk):
    return label_row - base == lax.broadcasted_iota(jnp.int32, (count, chunk), 0)


def label_row_of(digit_rows, count):
    d = digit_rows[:, :count].astype(jnp.float32)
    return (d[0:1] + 256.0 * d[1:2] + 65536.0 * d[2:3]).astype(jnp.int32)


def own_kernel(bases, scalars, img, txt, lab_col, part, img_in, txt_in, img_out, txt_out):
    add_meetings(((0, part),), bases, scalars, img, txt, lab_col, img_in, txt_in, img_out, txt_out)


def near_kernel(bases, scalars, img, txt, lab_col, near1, near2, near3, img_in, txt_in, img_out, txt_out):
    nears = ((1, near1), (2, near2), (3, near3))
    add_meetings(nears, bases, scalars, img, txt, lab_col, img_in, txt_in, img_out, txt_out)


def add_meetings(parts, bases, scalars, img, txt, lab_col, img_in, txt_in, img_out, txt_out):
    count = img.shape[0]
    chunk = (parts[0][1].shape[0] - DIGIT_ROWS) // 2
    scale, shift = scalars[0], scalars[1]
    img_total, txt_total = img_in[...], txt_in[...]
    for which, part in parts:
        hit = hit_columns(lab_col[...], bases[which] + bases[5], count, chunk)
        img_total += gradient(img[...], part[:chunk, :], hit, scale, shift)
        hit = hit_rows(label_row_of(part[2 * chunk :, :], chunk), bases[0], count, chunk)
        txt_total += gradient(txt[...], part[chunk : 2 * chunk, :], hit, scale, shift)
    img_out[...] = img_total
    txt_out[...] = txt_total


def far_texts_kernel(scalars, bases, img, lab_col, far_txt, img_in, image_grad):
    count = img.shape[0]
    scale, shift = scalars[0], scalars[1]
    hit = hit_columns(lab_col[...], bases[4], count, count)
    total = img_in[...] + gradient(img[...], far_txt[...], hit, scale, shift)
    image_grad[...] = (scale * total).astype(jnp.bfloat16)


def far_images_kernel(scalars, bases, txt, far_img, far_lab, txt_in, image_grad, text_grad, image_grad_out):
    count = txt.shape[0]
    scale, shift = scalars[0], scalars[1]
    hit = hit_rows(far_lab[...], bases[0], count, count)
    total = txt_in[...] + gradient(txt[...], far_img[...], hit, scale, shift)
    text_grad[...] = (scale * total).astype(jnp.bfloat16)


def cost(products, count, width):
    return pl.CostEstimate(
        flops=4 * products * count * count * width,
        bytes_accessed=6 * products * count * width,
        transcendentals=products * count * count,
    )


def local(images, texts, labels, log_scale, bias):
    count, width = images.shape
    pair_size = lax.axis_size("pair")
    far = lax.axis_size("dp").bit_length() - 2
    myself = lax.axis_index("dp") * pair_size + lax.axis_index("pair")

    anywhere = pl.BlockSpec(memory_space=pl.ANY)
    params = pltpu.CompilerParams(vmem_limit_bytes=VMEM_LIMIT)
    acc = jax.ShapeDtypeStruct((count, width), jnp.float32)
    out = jax.ShapeDtypeStruct((count, width), jnp.bfloat16)

    def kernel(body, out_shape, *args, passed=0, products=1):
        many = isinstance(out_shape, tuple)
        specs = [SMEM, SMEM] + [VMEM] * (len(args) - 2)
        out_specs = (VMEM,) * len(out_shape) if many else VMEM
        aliases = {len(args) - i: len(out_shape) - i for i in range(1, passed + 1)}
        if products == 0:
            specs[-1] = anywhere
            out_specs = out_specs[:-1] + (anywhere,)
        return pl.pallas_call(
            body,
            out_shape=out_shape,
            in_specs=specs,
            out_specs=out_specs,
            input_output_aliases=aliases,
            compiler_params=params,
            cost_estimate=cost(products, count, width),
            name=body.__name__,
        )(*args)

    digits = jnp.stack([labels & 255, (labels >> 8) & 255, labels >> 16]).astype(jnp.bfloat16)
    digits = jnp.pad(digits, ((0, DIGIT_ROWS - 3), (0, width - count)))
    second = RING // 2 - FIRST_STEPS
    far_txt = along_ring(along_ring(texts, FIRST_STEPS), second)
    far_img = along_ring(along_ring(images, FIRST_STEPS), second)
    far_lab = from_partner(labels.reshape(1, count), "dp", far)

    offsets = jnp.array([0, 1, pair_size, 2 * pair_size, pair_size << far], jnp.int32)
    bases = jnp.bitwise_xor(myself, offsets) * count
    scalars = jnp.concatenate([jnp.exp(log_scale), bias])
    lab_col = labels.reshape(count, 1)
    sums = (jnp.zeros((count, width), jnp.float32),) * 2
    chunk = count // CHUNKS

    def near(step, sums):
        at = step * chunk
        part = jnp.concatenate(
            [
                lax.dynamic_slice_in_dim(texts, at, chunk, 0),
                lax.dynamic_slice_in_dim(images, at, chunk, 0),
                jnp.pad(
                    lax.dynamic_slice_in_dim(digits, at, chunk, 1), ((0, 0), (0, width - chunk))
                ),
            ],
            axis=0,
        )
        arrived = [from_partner(part, axis, bit) for axis, bit in (("dp", 1), ("dp", 0), ("pair", 0))]
        here = jnp.concatenate([bases, jnp.reshape(at, (1,))])
        mine = (here, scalars, images, texts, lab_col)
        sums = kernel(own_kernel, (acc, acc), *mine, part, *sums, passed=2, products=2)
        return kernel(near_kernel, (acc, acc), *mine, *arrived[::-1], *sums, passed=2, products=3)

    img_acc, txt_acc = lax.fori_loop(0, CHUNKS, near, sums)
    image_grad = kernel(far_texts_kernel, out, scalars, bases, images, lab_col, far_txt, img_acc)
    text_grad, image_grad = kernel(
        far_images_kernel, (out, out), scalars, bases, texts, far_img, far_lab, txt_acc, image_grad, passed=1, products=0
    )
    return image_grad, text_grad


def solution(mesh):
    placed = (P(("dp", "pair"), None), P(("dp", "pair"), None), P(("dp", "pair")), P(), P())
    return jax.shard_map(
        local,
        mesh=mesh,
        in_specs=placed,
        out_specs=(P(("dp", "pair"), None), P(("dp", "pair"), None)),
        check_vma=False,
    )
```

```python
import jax
import jax.numpy as jnp
from jax import lax
from jax.experimental import pallas as pl
from jax.experimental.pallas import tpu as pltpu
from jax.sharding import PartitionSpec as P

VMEM = pl.BlockSpec(memory_space=pltpu.VMEM)
SMEM = pl.BlockSpec(memory_space=pltpu.SMEM)
DIGIT_ROWS = 16
CHUNKS = 2
RING = 16
FIRST_STEPS = 1
VMEM_LIMIT = 28 << 20


def from_partner(block, axis, bit):
    count = lax.axis_size(axis)
    return lax.ppermute(block, axis, [(i, i ^ (1 << bit)) for i in range(count)])


def along_ring(block, steps):
    axes = ("dp", "pair")
    count = lax.axis_size(axes)
    step = count // RING * steps
    return lax.ppermute(
        block, axes, [(i, (i + (step if i % 2 == 0 else -step)) % count) for i in range(count)]
    )


def gradient(rows, cols, hit, scale, shift):
    logits = scale * lax.dot_general(
        rows, cols, (((1,), (1,)), ((), ())), preferred_element_type=jnp.float32
    ) + shift
    coeff = (jax.nn.sigmoid(logits) - hit.astype(jnp.float32)).astype(jnp.bfloat16)
    return jnp.dot(coeff, cols, preferred_element_type=jnp.float32)


def hit_columns(label_column, base, count, chunk):
    return label_column - base == lax.broadcasted_iota(jnp.int32, (count, chunk), 1)


def hit_rows(label_row, base, count, chunk):
    return label_row - base == lax.broadcasted_iota(jnp.int32, (count, chunk), 0)


def label_row_of(digit_rows, count):
    d = digit_rows[:, :count].astype(jnp.float32)
    return (d[0:1] + 256.0 * d[1:2] + 65536.0 * d[2:3]).astype(jnp.int32)


def own_kernel(bases, scalars, img, txt, lab_col, part, img_in, txt_in, img_out, txt_out):
    add_meetings(((0, part),), bases, scalars, img, txt, lab_col, img_in, txt_in, img_out, txt_out)


def near_kernel(bases, scalars, img, txt, lab_col, near1, near2, near3, img_in, txt_in, img_out, txt_out):
    nears = ((1, near1), (2, near2), (3, near3))
    add_meetings(nears, bases, scalars, img, txt, lab_col, img_in, txt_in, img_out, txt_out)


def add_meetings(parts, bases, scalars, img, txt, lab_col, img_in, txt_in, img_out, txt_out):
    count = img.shape[0]
    chunk = (parts[0][1].shape[0] - DIGIT_ROWS) // 2
    scale, shift = scalars[0], scalars[1]
    img_total, txt_total = img_in[...], txt_in[...]
    for which, part in parts:
        hit = hit_columns(lab_col[...], bases[which] + bases[5], count, chunk)
        img_total += gradient(img[...], part[:chunk, :], hit, scale, shift)
        hit = hit_rows(label_row_of(part[2 * chunk :, :], chunk), bases[0], count, chunk)
        txt_total += gradient(txt[...], part[chunk : 2 * chunk, :], hit, scale, shift)
    img_out[...] = img_total
    txt_out[...] = txt_total


def far_texts_kernel(scalars, bases, img, lab_col, far_txt, img_in, image_grad):
    count = img.shape[0]
    scale, shift = scalars[0], scalars[1]
    hit = hit_columns(lab_col[...], bases[4], count, count)
    total = img_in[...] + gradient(img[...], far_txt[...], hit, scale, shift)
    image_grad[...] = (scale * total).astype(jnp.bfloat16)


def far_images_kernel(scalars, bases, txt, far_img, far_lab, txt_in, image_grad, text_grad, image_grad_out):
    count = txt.shape[0]
    scale, shift = scalars[0], scalars[1]
    their_lab = jnp.where(bases[4] < bases[0], far_lab[0:1, :], far_lab[1:2, :])
    hit = hit_rows(their_lab, bases[0], count, count)
    total = txt_in[...] + gradient(txt[...], far_img[...], hit, scale, shift)
    text_grad[...] = (scale * total).astype(jnp.bfloat16)


def cost(products, count, width):
    return pl.CostEstimate(
        flops=4 * products * count * count * width,
        bytes_accessed=6 * products * count * width,
        transcendentals=products * count * count,
    )


def local(images, texts, labels, log_scale, bias):
    count, width = images.shape
    pair_size = lax.axis_size("pair")
    far = lax.axis_size("dp").bit_length() - 2
    myself = lax.axis_index("dp") * pair_size + lax.axis_index("pair")

    anywhere = pl.BlockSpec(memory_space=pl.ANY)
    params = pltpu.CompilerParams(vmem_limit_bytes=VMEM_LIMIT)
    acc = jax.ShapeDtypeStruct((count, width), jnp.float32)
    out = jax.ShapeDtypeStruct((count, width), jnp.bfloat16)

    def kernel(body, out_shape, *args, passed=0, products=1):
        many = isinstance(out_shape, tuple)
        specs = [SMEM, SMEM] + [VMEM] * (len(args) - 2)
        out_specs = (VMEM,) * len(out_shape) if many else VMEM
        aliases = {len(args) - i: len(out_shape) - i for i in range(1, passed + 1)}
        if products == 0:
            specs[-1] = anywhere
            out_specs = out_specs[:-1] + (anywhere,)
        return pl.pallas_call(
            body,
            out_shape=out_shape,
            in_specs=specs,
            out_specs=out_specs,
            input_output_aliases=aliases,
            compiler_params=params,
            cost_estimate=cost(products, count, width),
            name=body.__name__,
        )(*args)

    digits = jnp.stack([labels & 255, (labels >> 8) & 255, labels >> 16]).astype(jnp.bfloat16)
    digits = jnp.pad(digits, ((0, DIGIT_ROWS - 3), (0, width - count)))
    second = RING // 2 - FIRST_STEPS
    far_txt = along_ring(along_ring(texts, FIRST_STEPS), second)
    far_img = along_ring(along_ring(images, FIRST_STEPS), second)
    half = 1 << far
    far_lab = lax.all_gather(
        labels, "dp", axis_index_groups=[[i, i + half] for i in range(half)], axis=0
    )

    offsets = jnp.array([0, 1, pair_size, 2 * pair_size, pair_size << far], jnp.int32)
    bases = jnp.bitwise_xor(myself, offsets) * count
    scalars = jnp.concatenate([jnp.exp(log_scale), bias])
    lab_col = labels.reshape(count, 1)
    sums = (jnp.zeros((count, width), jnp.float32),) * 2
    chunk = count // CHUNKS

    def near(step, sums):
        at = step * chunk
        part = jnp.concatenate(
            [
                lax.dynamic_slice_in_dim(texts, at, chunk, 0),
                lax.dynamic_slice_in_dim(images, at, chunk, 0),
                jnp.pad(
                    lax.dynamic_slice_in_dim(digits, at, chunk, 1), ((0, 0), (0, width - chunk))
                ),
            ],
            axis=0,
        )
        arrived = [from_partner(part, axis, bit) for axis, bit in (("dp", 1), ("dp", 0), ("pair", 0))]
        here = jnp.concatenate([bases, jnp.reshape(at, (1,))])
        mine = (here, scalars, images, texts, lab_col)
        sums = kernel(own_kernel, (acc, acc), *mine, part, *sums, passed=2, products=2)
        return kernel(near_kernel, (acc, acc), *mine, *arrived[::-1], *sums, passed=2, products=3)

    img_acc, txt_acc = lax.fori_loop(0, CHUNKS, near, sums)
    image_grad = kernel(far_texts_kernel, out, scalars, bases, images, lab_col, far_txt, img_acc)
    text_grad, image_grad = kernel(
        far_images_kernel, (out, out), scalars, bases, texts, far_img, far_lab, txt_acc, image_grad, passed=1, products=0
    )
    return image_grad, text_grad


def solution(mesh):
    placed = (P(("dp", "pair"), None), P(("dp", "pair"), None), P(("dp", "pair")), P(), P())
    return jax.shard_map(
        local,
        mesh=mesh,
        in_specs=placed,
        out_specs=(P(("dp", "pair"), None), P(("dp", "pair"), None)),
        check_vma=False,
    )
```

```python
import jax
import jax.numpy as jnp
from jax import lax
from jax.experimental import pallas as pl
from jax.experimental.pallas import tpu as pltpu
from jax.sharding import PartitionSpec as P

VMEM = pl.BlockSpec(memory_space=pltpu.VMEM)
SMEM = pl.BlockSpec(memory_space=pltpu.SMEM)
DIGIT_ROWS = 16
CHUNKS = 2
RING = 16
FIRST_STEPS = 1
VMEM_LIMIT = 28 << 20


def from_partner(block, axis, bit):
    count = lax.axis_size(axis)
    return lax.ppermute(block, axis, [(i, i ^ (1 << bit)) for i in range(count)])


def along_ring(block, steps):
    axes = ("dp", "pair")
    count = lax.axis_size(axes)
    step = count // RING * steps
    return lax.ppermute(
        block, axes, [(i, (i + (step if i % 2 == 0 else -step)) % count) for i in range(count)]
    )


def gradient(rows, cols, hit, scale, shift):
    logits = scale * lax.dot_general(
        rows, cols, (((1,), (1,)), ((), ())), preferred_element_type=jnp.float32
    ) + shift
    coeff = (jax.nn.sigmoid(logits) - hit.astype(jnp.float32)).astype(jnp.bfloat16)
    return jnp.dot(coeff, cols, preferred_element_type=jnp.float32)


def hit_columns(label_column, base, count, chunk):
    return label_column - base == lax.broadcasted_iota(jnp.int32, (count, chunk), 1)


def hit_rows(label_row, base, count, chunk):
    return label_row - base == lax.broadcasted_iota(jnp.int32, (count, chunk), 0)


def label_row_of(digit_rows, count):
    d = digit_rows[:, :count].astype(jnp.float32)
    return (d[0:1] + 256.0 * d[1:2] + 65536.0 * d[2:3]).astype(jnp.int32)


def own_kernel(bases, scalars, img, txt, lab_col, part, img_in, txt_in, img_out, txt_out):
    add_meetings(((0, part),), bases, scalars, img, txt, lab_col, img_in, txt_in, img_out, txt_out)


def near_kernel(bases, scalars, img, txt, lab_col, near1, near2, near3, img_in, txt_in, img_out, txt_out):
    nears = ((1, near1), (2, near2), (3, near3))
    add_meetings(nears, bases, scalars, img, txt, lab_col, img_in, txt_in, img_out, txt_out)


def add_meetings(parts, bases, scalars, img, txt, lab_col, img_in, txt_in, img_out, txt_out):
    count = img.shape[0]
    chunk = (parts[0][1].shape[0] - DIGIT_ROWS) // 2
    scale, shift = scalars[0], scalars[1]
    img_total, txt_total = img_in[...], txt_in[...]
    for which, part in parts:
        hit = hit_columns(lab_col[...], bases[which] + bases[5], count, chunk)
        img_total += gradient(img[...], part[:chunk, :], hit, scale, shift)
        hit = hit_rows(label_row_of(part[2 * chunk :, :], chunk), bases[0], count, chunk)
        txt_total += gradient(txt[...], part[chunk : 2 * chunk, :], hit, scale, shift)
    img_out[...] = img_total
    txt_out[...] = txt_total


def far_texts_kernel(scalars, bases, img, lab_col, far_txt, img_in, image_grad):
    count = img.shape[0]
    scale, shift = scalars[0], scalars[1]
    hit = hit_columns(lab_col[...], bases[4], count, count)
    total = img_in[...] + gradient(img[...], far_txt[...], hit, scale, shift)
    image_grad[...] = (scale * total).astype(jnp.bfloat16)


def far_images_kernel(scalars, bases, txt, far_img, far_lab, txt_in, image_grad, text_grad, image_grad_out):
    count = txt.shape[0]
    scale, shift = scalars[0], scalars[1]
    hit = hit_rows(far_lab[...], bases[0], count, count)
    total = txt_in[...] + gradient(txt[...], far_img[...], hit, scale, shift)
    text_grad[...] = (scale * total).astype(jnp.bfloat16)


def cost(products, count, width):
    return pl.CostEstimate(
        flops=4 * products * count * count * width,
        bytes_accessed=6 * products * count * width,
        transcendentals=products * count * count,
    )


def local(images, texts, labels, log_scale, bias):
    count, width = images.shape
    pair_size = lax.axis_size("pair")
    far = lax.axis_size("dp").bit_length() - 2
    myself = lax.axis_index("dp") * pair_size + lax.axis_index("pair")

    anywhere = pl.BlockSpec(memory_space=pl.ANY)
    params = pltpu.CompilerParams(vmem_limit_bytes=VMEM_LIMIT)
    acc = jax.ShapeDtypeStruct((count, width), jnp.float32)
    out = jax.ShapeDtypeStruct((count, width), jnp.bfloat16)

    def kernel(body, out_shape, *args, passed=0, products=0, last_stays=False):
        many = isinstance(out_shape, tuple)
        specs = [SMEM, SMEM] + [VMEM] * (len(args) - 2)
        out_specs = (VMEM,) * len(out_shape) if many else VMEM
        aliases = {len(args) - i: len(out_shape) - i for i in range(1, passed + 1)}
        if last_stays:
            specs[-1] = anywhere
            out_specs = out_specs[:-1] + (anywhere,)
        return pl.pallas_call(
            body,
            out_shape=out_shape,
            in_specs=specs,
            out_specs=out_specs,
            input_output_aliases=aliases,
            compiler_params=params,
            cost_estimate=cost(products, count, width),
            name=body.__name__,
        )(*args)

    digits = jnp.stack([labels & 255, (labels >> 8) & 255, labels >> 16]).astype(jnp.bfloat16)
    digits = jnp.pad(digits, ((0, DIGIT_ROWS - 3), (0, width - count)))
    second = RING // 2 - FIRST_STEPS
    far_txt = along_ring(along_ring(texts, FIRST_STEPS), second)
    far_img = along_ring(along_ring(images, FIRST_STEPS), second)
    far_lab = from_partner(labels.reshape(1, count), "dp", far)

    offsets = jnp.array([0, 1, pair_size, 2 * pair_size, pair_size << far], jnp.int32)
    bases = jnp.bitwise_xor(myself, offsets) * count
    scalars = jnp.concatenate([jnp.exp(log_scale), bias])
    lab_col = labels.reshape(count, 1)
    chunk = count // CHUNKS
    sums = (jnp.zeros((count, width), jnp.float32),) * 2
    nothing = (jnp.zeros((2 * chunk + DIGIT_ROWS, width), jnp.bfloat16),) * 3

    def meet(body, at, parts, sums, products):
        here = jnp.concatenate([bases, jnp.reshape(at, (1,))])
        args = (here, scalars, images, texts, lab_col, *parts, *sums)
        return kernel(body, (acc, acc), *args, passed=2, products=products)

    def near(step, state):
        before, sums = state
        at = step * chunk
        part = jnp.concatenate(
            [
                lax.dynamic_slice_in_dim(texts, at, chunk, 0),
                lax.dynamic_slice_in_dim(images, at, chunk, 0),
                jnp.pad(
                    lax.dynamic_slice_in_dim(digits, at, chunk, 1), ((0, 0), (0, width - chunk))
                ),
            ],
            axis=0,
        )
        arrived = [from_partner(part, axis, bit) for axis, bit in (("dp", 1), ("dp", 0), ("pair", 0))]
        sums = meet(own_kernel, at, (part,), sums, 1)
        sums = meet(near_kernel, at - chunk, before, sums, 3)
        return tuple(arrived[::-1]), tuple(sums)

    arrived, sums = lax.fori_loop(0, CHUNKS, near, (nothing, sums))
    img_acc, txt_acc = meet(near_kernel, jnp.int32((CHUNKS - 1) * chunk), arrived, sums, 0)
    image_grad = kernel(far_texts_kernel, out, scalars, bases, images, lab_col, far_txt, img_acc)
    text_grad, image_grad = kernel(
        far_images_kernel, (out, out), scalars, bases, texts, far_img, far_lab, txt_acc, image_grad,
        passed=1, last_stays=True,
    )
    return image_grad, text_grad


def solution(mesh):
    placed = (P(("dp", "pair"), None), P(("dp", "pair"), None), P(("dp", "pair")), P(), P())
    return jax.shard_map(
        local,
        mesh=mesh,
        in_specs=placed,
        out_specs=(P(("dp", "pair"), None), P(("dp", "pair"), None)),
        check_vma=False,
    )
```

```python
import jax
import jax.numpy as jnp
from jax import lax
from jax.experimental import pallas as pl
from jax.experimental.pallas import tpu as pltpu
from jax.sharding import PartitionSpec as P

VMEM = pl.BlockSpec(memory_space=pltpu.VMEM)
SMEM = pl.BlockSpec(memory_space=pltpu.SMEM)
DIGIT_ROWS = 16
CHUNKS = 2
RING = 16
FIRST_STEPS = 1
VMEM_LIMIT = 28 << 20


def from_partner(block, axis, bit):
    count = lax.axis_size(axis)
    return lax.ppermute(block, axis, [(i, i ^ (1 << bit)) for i in range(count)])


def along_ring(block, steps):
    axes = ("dp", "pair")
    count = lax.axis_size(axes)
    step = count // RING * steps
    return lax.ppermute(
        block, axes, [(i, (i + (step if i % 2 == 0 else -step)) % count) for i in range(count)]
    )


def gradient(rows, cols, hit, scale, shift):
    logits = scale * lax.dot_general(
        rows, cols, (((1,), (1,)), ((), ())), preferred_element_type=jnp.float32
    ) + shift
    coeff = (jax.nn.sigmoid(logits) - hit.astype(jnp.float32)).astype(jnp.bfloat16)
    return jnp.dot(coeff, cols, preferred_element_type=jnp.float32)


def hit_columns(label_column, base, count, chunk):
    return label_column - base == lax.broadcasted_iota(jnp.int32, (count, chunk), 1)


def hit_rows(label_row, base, count, chunk):
    return label_row - base == lax.broadcasted_iota(jnp.int32, (count, chunk), 0)


def label_row_of(digit_rows, count):
    d = digit_rows[:, :count].astype(jnp.float32)
    return (d[0:1] + 256.0 * d[1:2] + 65536.0 * d[2:3]).astype(jnp.int32)


def own_kernel(bases, scalars, img, txt, lab_col, part, img_in, txt_in, img_out, txt_out):
    add_meetings(((0, part),), bases, scalars, img, txt, lab_col, img_in, txt_in, img_out, txt_out)


def near_kernel(bases, scalars, img, txt, lab_col, near1, near2, near3, img_in, txt_in, img_out, txt_out):
    nears = ((1, near1), (2, near2), (3, near3))
    add_meetings(nears, bases, scalars, img, txt, lab_col, img_in, txt_in, img_out, txt_out)


def add_meetings(parts, bases, scalars, img, txt, lab_col, img_in, txt_in, img_out, txt_out):
    count = img.shape[0]
    chunk = (parts[0][1].shape[0] - DIGIT_ROWS) // 2
    scale, shift = scalars[0], scalars[1]
    img_total, txt_total = img_in[...], txt_in[...]
    for which, part in parts:
        hit = hit_columns(lab_col[...], bases[which] + bases[5], count, chunk)
        img_total += gradient(img[...], part[:chunk, :], hit, scale, shift)
        hit = hit_rows(label_row_of(part[2 * chunk :, :], chunk), bases[0], count, chunk)
        txt_total += gradient(txt[...], part[chunk : 2 * chunk, :], hit, scale, shift)
    img_out[...] = img_total
    txt_out[...] = txt_total


def pass_kernel(scalars, bases, txt_in, nearly_img, out):
    pass


def far_texts_kernel(scalars, bases, img, lab_col, far_txt, img_in, image_grad):
    count = img.shape[0]
    scale, shift = scalars[0], scalars[1]
    hit = hit_columns(lab_col[...], bases[4], count, count)
    total = img_in[...] + gradient(img[...], far_txt[...], hit, scale, shift)
    image_grad[...] = (scale * total).astype(jnp.bfloat16)


def far_images_kernel(scalars, bases, txt, far_img, far_lab, txt_in, image_grad, text_grad, image_grad_out):
    count = txt.shape[0]
    scale, shift = scalars[0], scalars[1]
    hit = hit_rows(far_lab[...], bases[0], count, count)
    total = txt_in[...] + gradient(txt[...], far_img[...], hit, scale, shift)
    text_grad[...] = (scale * total).astype(jnp.bfloat16)


def cost(products, count, width):
    return pl.CostEstimate(
        flops=4 * products * count * count * width,
        bytes_accessed=6 * products * count * width,
        transcendentals=products * count * count,
    )


def local(images, texts, labels, log_scale, bias):
    count, width = images.shape
    pair_size = lax.axis_size("pair")
    far = lax.axis_size("dp").bit_length() - 2
    myself = lax.axis_index("dp") * pair_size + lax.axis_index("pair")

    anywhere = pl.BlockSpec(memory_space=pl.ANY)
    params = pltpu.CompilerParams(vmem_limit_bytes=VMEM_LIMIT)
    acc = jax.ShapeDtypeStruct((count, width), jnp.float32)
    out = jax.ShapeDtypeStruct((count, width), jnp.bfloat16)

    def kernel(body, out_shape, *args, passed=0, products=0, last_stays=False):
        many = isinstance(out_shape, tuple)
        specs = [SMEM, SMEM] + [VMEM] * (len(args) - 2)
        out_specs = (VMEM,) * len(out_shape) if many else VMEM
        aliases = {len(args) - i: len(out_shape) - i for i in range(1, passed + 1)}
        if last_stays:
            specs[-1] = anywhere
            out_specs = out_specs[:-1] + (anywhere,)
        return pl.pallas_call(
            body,
            out_shape=out_shape,
            in_specs=specs,
            out_specs=out_specs,
            input_output_aliases=aliases,
            compiler_params=params,
            cost_estimate=cost(products, count, width),
            name=body.__name__,
        )(*args)

    digits = jnp.stack([labels & 255, (labels >> 8) & 255, labels >> 16]).astype(jnp.bfloat16)
    digits = jnp.pad(digits, ((0, DIGIT_ROWS - 3), (0, width - count)))
    second = RING // 2 - FIRST_STEPS
    far_txt = along_ring(along_ring(texts, FIRST_STEPS), second)
    nearly_img = along_ring(images, second)
    far_lab = from_partner(labels.reshape(1, count), "dp", far)

    offsets = jnp.array([0, 1, pair_size, 2 * pair_size, pair_size << far], jnp.int32)
    bases = jnp.bitwise_xor(myself, offsets) * count
    scalars = jnp.concatenate([jnp.exp(log_scale), bias])
    lab_col = labels.reshape(count, 1)
    chunk = count // CHUNKS
    sums = (jnp.zeros((count, width), jnp.float32),) * 2
    nothing = (jnp.zeros((2 * chunk + DIGIT_ROWS, width), jnp.bfloat16),) * 3

    def meet(body, at, parts, sums, products):
        here = jnp.concatenate([bases, jnp.reshape(at, (1,))])
        args = (here, scalars, images, texts, lab_col, *parts, *sums)
        return kernel(body, (acc, acc), *args, passed=2, products=products)

    def near(step, state):
        before, sums = state
        at = step * chunk
        part = jnp.concatenate(
            [
                lax.dynamic_slice_in_dim(texts, at, chunk, 0),
                lax.dynamic_slice_in_dim(images, at, chunk, 0),
                jnp.pad(
                    lax.dynamic_slice_in_dim(digits, at, chunk, 1), ((0, 0), (0, width - chunk))
                ),
            ],
            axis=0,
        )
        arrived = [from_partner(part, axis, bit) for axis, bit in (("dp", 1), ("dp", 0), ("pair", 0))]
        sums = meet(own_kernel, at, (part,), sums, 1)
        sums = meet(near_kernel, at - chunk, before, sums, 3)
        return tuple(arrived[::-1]), tuple(sums)

    arrived, sums = lax.fori_loop(0, CHUNKS, near, (nothing, sums))
    anywhere_in = [SMEM, SMEM, anywhere, anywhere]
    nearly_img = pl.pallas_call(
        pass_kernel,
        out_shape=out,
        in_specs=anywhere_in,
        out_specs=anywhere,
        input_output_aliases={3: 0},
        compiler_params=params,
        cost_estimate=cost(0, count, width),
        name="pass_kernel",
    )(scalars, bases, sums[1], nearly_img)
    far_img = along_ring(nearly_img, FIRST_STEPS)
    img_acc, txt_acc = meet(near_kernel, jnp.int32((CHUNKS - 1) * chunk), arrived, sums, 0)
    image_grad = kernel(far_texts_kernel, out, scalars, bases, images, lab_col, far_txt, img_acc)
    text_grad, image_grad = kernel(
        far_images_kernel, (out, out), scalars, bases, texts, far_img, far_lab, txt_acc, image_grad,
        passed=1, last_stays=True,
    )
    return image_grad, text_grad


def solution(mesh):
    placed = (P(("dp", "pair"), None), P(("dp", "pair"), None), P(("dp", "pair")), P(), P())
    return jax.shard_map(
        local,
        mesh=mesh,
        in_specs=placed,
        out_specs=(P(("dp", "pair"), None), P(("dp", "pair"), None)),
        check_vma=False,
    )
```

```python
import jax
import jax.numpy as jnp
from jax import lax
from jax.experimental import pallas as pl
from jax.experimental.pallas import tpu as pltpu
from jax.sharding import PartitionSpec as P

VMEM = pl.BlockSpec(memory_space=pltpu.VMEM)
SMEM = pl.BlockSpec(memory_space=pltpu.SMEM)
DIGIT_ROWS = 16
CHUNKS = 2
RING = 16
FIRST_STEPS = 1
VMEM_LIMIT = 22 << 20


def from_partner(block, axis, bit):
    count = lax.axis_size(axis)
    return lax.ppermute(block, axis, [(i, i ^ (1 << bit)) for i in range(count)])


def along_ring(block, steps):
    axes = ("dp", "pair")
    count = lax.axis_size(axes)
    step = count // RING * steps
    return lax.ppermute(
        block, axes, [(i, (i + (step if i % 2 == 0 else -step)) % count) for i in range(count)]
    )


def gradient(rows, cols, hit, scale, shift):
    logits = scale * lax.dot_general(
        rows, cols, (((1,), (1,)), ((), ())), preferred_element_type=jnp.float32
    ) + shift
    coeff = (jax.nn.sigmoid(logits) - hit.astype(jnp.float32)).astype(jnp.bfloat16)
    return jnp.dot(coeff, cols, preferred_element_type=jnp.float32)


def hit_columns(label_column, base, count, chunk):
    return label_column - base == lax.broadcasted_iota(jnp.int32, (count, chunk), 1)


def hit_rows(label_row, base, count, chunk):
    return label_row - base == lax.broadcasted_iota(jnp.int32, (count, chunk), 0)


def label_row_of(digit_rows, count):
    d = digit_rows[:, :count].astype(jnp.float32)
    return (d[0:1] + 256.0 * d[1:2] + 65536.0 * d[2:3]).astype(jnp.int32)


def own_kernel(bases, scalars, img, txt, lab_col, part, img_in, txt_in, img_out, txt_out):
    add_meetings(((0, part),), bases, scalars, img, txt, lab_col, img_in, txt_in, img_out, txt_out)


def near_kernel(bases, scalars, img, txt, lab_col, near1, near2, near3, img_in, txt_in, img_out, txt_out):
    nears = ((1, near1), (2, near2), (3, near3))
    add_meetings(nears, bases, scalars, img, txt, lab_col, img_in, txt_in, img_out, txt_out)


def add_meetings(parts, bases, scalars, img, txt, lab_col, img_in, txt_in, img_out, txt_out):
    count = img.shape[0]
    chunk = (parts[0][1].shape[0] - DIGIT_ROWS) // 2
    scale, shift = scalars[0], scalars[1]
    img_total, txt_total = img_in[...], txt_in[...]
    for which, part in parts:
        hit = hit_columns(lab_col[...], bases[which] + bases[5], count, chunk)
        img_total += gradient(img[...], part[:chunk, :], hit, scale, shift)
        hit = hit_rows(label_row_of(part[2 * chunk :, :], chunk), bases[0], count, chunk)
        txt_total += gradient(txt[...], part[chunk : 2 * chunk, :], hit, scale, shift)
    img_out[...] = img_total
    txt_out[...] = txt_total


def far_texts_kernel(scalars, bases, img, lab_col, far_txt, img_in, image_grad):
    count = img.shape[0]
    scale, shift = scalars[0], scalars[1]
    hit = hit_columns(lab_col[...], bases[4], count, count)
    total = img_in[...] + gradient(img[...], far_txt[...], hit, scale, shift)
    image_grad[...] = (scale * total).astype(jnp.bfloat16)


def far_images_kernel(scalars, bases, txt, far_img, far_lab, txt_in, image_grad, text_grad, image_grad_out):
    count = txt.shape[0]
    scale, shift = scalars[0], scalars[1]
    hit = hit_rows(far_lab[...], bases[0], count, count)
    total = txt_in[...] + gradient(txt[...], far_img[...], hit, scale, shift)
    text_grad[...] = (scale * total).astype(jnp.bfloat16)


def cost(products, count, width):
    return pl.CostEstimate(
        flops=4 * products * count * count * width,
        bytes_accessed=6 * products * count * width,
        transcendentals=products * count * count,
    )


def local(images, texts, labels, log_scale, bias):
    count, width = images.shape
    pair_size = lax.axis_size("pair")
    far = lax.axis_size("dp").bit_length() - 2
    myself = lax.axis_index("dp") * pair_size + lax.axis_index("pair")

    anywhere = pl.BlockSpec(memory_space=pl.ANY)
    params = pltpu.CompilerParams(vmem_limit_bytes=VMEM_LIMIT)
    acc = jax.ShapeDtypeStruct((count, width), jnp.float32)
    out = jax.ShapeDtypeStruct((count, width), jnp.bfloat16)

    def kernel(body, out_shape, *args, passed=0, products=0, last_stays=False):
        many = isinstance(out_shape, tuple)
        specs = [SMEM, SMEM] + [VMEM] * (len(args) - 2)
        out_specs = (VMEM,) * len(out_shape) if many else VMEM
        aliases = {len(args) - i: len(out_shape) - i for i in range(1, passed + 1)}
        if last_stays:
            specs[-1] = anywhere
            out_specs = out_specs[:-1] + (anywhere,)
        return pl.pallas_call(
            body,
            out_shape=out_shape,
            in_specs=specs,
            out_specs=out_specs,
            input_output_aliases=aliases,
            compiler_params=params,
            cost_estimate=cost(products, count, width),
            name=body.__name__,
        )(*args)

    digits = jnp.stack([labels & 255, (labels >> 8) & 255, labels >> 16]).astype(jnp.bfloat16)
    digits = jnp.pad(digits, ((0, DIGIT_ROWS - 3), (0, width - count)))
    second = RING // 2 - FIRST_STEPS
    far_txt = along_ring(along_ring(texts, FIRST_STEPS), second)
    far_img = along_ring(along_ring(images, FIRST_STEPS), second)
    far_lab = from_partner(labels.reshape(1, count), "dp", far)

    offsets = jnp.array([0, 1, pair_size, 2 * pair_size, pair_size << far], jnp.int32)
    bases = jnp.bitwise_xor(myself, offsets) * count
    scalars = jnp.concatenate([jnp.exp(log_scale), bias])
    lab_col = labels.reshape(count, 1)
    chunk = count // CHUNKS
    sums = (jnp.zeros((count, width), jnp.float32),) * 2
    nothing = (jnp.zeros((2 * chunk + DIGIT_ROWS, width), jnp.bfloat16),) * 3

    def meet(body, at, parts, sums, products):
        here = jnp.concatenate([bases, jnp.reshape(at, (1,))])
        args = (here, scalars, images, texts, lab_col, *parts, *sums)
        return kernel(body, (acc, acc), *args, passed=2, products=products)

    def near(step, state):
        before, sums = state
        at = step * chunk
        part = jnp.concatenate(
            [
                lax.dynamic_slice_in_dim(texts, at, chunk, 0),
                lax.dynamic_slice_in_dim(images, at, chunk, 0),
                jnp.pad(
                    lax.dynamic_slice_in_dim(digits, at, chunk, 1), ((0, 0), (0, width - chunk))
                ),
            ],
            axis=0,
        )
        arrived = [from_partner(part, axis, bit) for axis, bit in (("dp", 1), ("dp", 0), ("pair", 0))]
        sums = meet(own_kernel, at, (part,), sums, 1)
        sums = meet(near_kernel, at - chunk, before, sums, 3)
        return tuple(arrived[::-1]), tuple(sums)

    arrived, sums = lax.fori_loop(0, CHUNKS, near, (nothing, sums))
    img_acc, txt_acc = meet(near_kernel, jnp.int32((CHUNKS - 1) * chunk), arrived, sums, 0)
    image_grad = kernel(far_texts_kernel, out, scalars, bases, images, lab_col, far_txt, img_acc)
    text_grad, image_grad = kernel(
        far_images_kernel, (out, out), scalars, bases, texts, far_img, far_lab, txt_acc, image_grad,
        passed=1, last_stays=True,
    )
    return image_grad, text_grad


def solution(mesh):
    placed = (P(("dp", "pair"), None), P(("dp", "pair"), None), P(("dp", "pair")), P(), P())
    return jax.shard_map(
        local,
        mesh=mesh,
        in_specs=placed,
        out_specs=(P(("dp", "pair"), None), P(("dp", "pair"), None)),
        check_vma=False,
    )
```
